128 devices in a mesh: ctx: 8 (over y_hi, z), tp: 4 (over x), req: 4 (over y_lo, core).
Axes of the slice: x: 4, y: 4 (y_hi: 2, y_lo: 2; y = y_hi * 2 + y_lo), z: 4, core: 2. Of those that a mesh axis runs over, the one named last changes fastest.
Arguments:
- queries: bfloat16 [256, 8, 8192], P('ctx', 'req', 'tp'), parts along dimension 1, may hold values from -5 to 5
- key_cache: bfloat16 [24576, 8, 512], P('ctx', 'req', 'tp'), parts along dimension 1, may hold values from -10 to 10
- value_cache: bfloat16 [24576, 8, 512], P('ctx', 'req', 'tp'), parts along dimension 1, may hold values from -6 to 6
- ctx_len: int32 [8], P('req'), parts along dimension 0, may hold values from 6080 to 24320, as said below
- new_count: int32 [8], P('req'), parts along dimension 0, may hold values from 64 to 256, as said below
Outputs:
- attended_out: bfloat16 [256, 8, 8192], P(('ctx', 'tp'), 'req'), parts along dimension 1
The draws below stay inside these ranges and needn't reach their ends.
There are 4 independent parts, one for each index of `req`. The reference program is written for one: setup_inputs(seed, part) draws one part's arguments, and reference() takes and returns one part's arrays. A program takes and returns all parts, laid end to end along the dimension named above; each array names one. Nothing has to cross between parts.
Inputs may be any that keep to these rules, and one draw needn't show every extreme that they name: `ctx_len`: some request has exactly 24320 cached tokens. Some request has exactly 256 new tokens; the slots ctx_len to ctx_len + new_count - 1 hold the new tokens' keys and values.
All inputs are finite; a program needn't handle non-finite values.
Results may differ from the reference program's by a relative error of at most 0.0075.
Values may be sent and summed in bfloat16 or wider, within the bound.
No kernel may reach another device: no remote copies, remote signals or barrier semaphores. Data moves between devices by JAX's collectives and lax.ppermute only.
A program may use at most 256 MiB of HBM per device.

```python
import jax
import jax.numpy as jnp
from jax import lax

H = 64
KVH = 4
HD = 128
GROUP = 16
NEWQ = 256
REQS = 2
SLOT = 24576


def draw_queries(key, part):
    key = jax.random.fold_in(key, 101)
    drawn = jax.random.normal(key, (NEWQ, REQS, H * HD), jnp.float32)
    return jnp.clip(drawn, -5.0, 5.0).astype(jnp.bfloat16)


def draw_key_cache(key, part):
    key = jax.random.fold_in(key, 202)
    drawn = 2.5 * jax.random.normal(key, (SLOT, REQS, KVH * HD), jnp.float32)
    return jnp.clip(drawn, -10.0, 10.0).astype(jnp.bfloat16)


def draw_ctx_len(key, part):
    key = jax.random.fold_in(key, 303)
    first_key, second_key = jax.random.split(key)
    lowest = max(1, (SLOT - NEWQ) // 4)
    longest = SLOT - NEWQ
    drawn = jax.random.randint(first_key, (REQS,), lowest, longest + 1, jnp.int32)
    order = jax.random.permutation(second_key, REQS)
    return jnp.where(order == 0, longest, drawn).astype(jnp.int32)


def draw_new_count(key, part):
    key = jax.random.fold_in(key, 404)
    first_key, second_key = jax.random.split(key)
    drawn = jax.random.randint(first_key, (REQS,), NEWQ // 4, NEWQ, jnp.int32)
    order = jax.random.permutation(second_key, REQS)
    return jnp.where(order == 0, NEWQ, drawn).astype(jnp.int32)


def block_scale(key, extent, shards, least, top_value):
    def one(axis_at, parts):
        steps = jax.random.uniform(jax.random.fold_in(jax.random.fold_in(key, 6), axis_at), (parts,), jnp.float32, least / len(shards), top_value / len(shards))
        return jnp.repeat(jnp.exp(steps), extent[axis_at] // parts).reshape((-1,) + (1,) * (len(extent) - axis_at - 1))

    gain = one(*shards[0])
    for cut in shards[1:]:
        gain = gain * one(*cut)
    return gain


def bell_draw(own_key, extent, spread, most, cuts=(), kind=jnp.bfloat16):
    result = spread * jax.random.normal(own_key, extent, jnp.float32)
    if cuts:
        result = result * block_scale(own_key, extent, cuts, -0.22, 0.18)
    return jnp.clip(result, -most, most).astype(kind)


def setup_inputs(seed: int = 0, part: int = 0) -> dict:
    key_of = jax.random.split(jax.random.key(seed), 6)
    own_keys = jax.random.split(jax.random.fold_in(key_of[5], part), 6)
    return {
        "queries": draw_queries(jax.random.fold_in(jax.random.fold_in(key_of[5], part), 71), part),
        "key_cache": draw_key_cache(jax.random.fold_in(jax.random.fold_in(key_of[5], part), 71), part),
        "value_cache": bell_draw(own_keys[2], (SLOT, REQS, KVH * HD), 1.0, 6.0, ((0, 8), (2, 4))),
        "ctx_len": draw_ctx_len(jax.random.fold_in(jax.random.fold_in(key_of[5], part), 71), part),
        "new_count": draw_new_count(jax.random.fold_in(jax.random.fold_in(key_of[5], part), 71), part),
    }


def reference(queries, key_cache, value_cache, ctx_len, new_count):
    results = []
    key_pos = jnp.arange(SLOT, dtype=jnp.int32)
    for request in range(REQS):
        query_heads = queries[:, request].reshape(NEWQ, H, HD).transpose(1, 0, 2).astype(jnp.float32)
        key_heads = key_cache[:, request].reshape(SLOT, KVH, HD).transpose(1, 0, 2).astype(jnp.float32)
        value_heads = value_cache[:, request].reshape(SLOT, KVH, HD).transpose(1, 0, 2)
        query_pos = ctx_len[request] + jnp.arange(NEWQ, dtype=jnp.int32)
        visible = key_pos[None, :] <= query_pos[:, None]

        def one_head(head):
            shared = head // GROUP
            scores = jnp.dot(query_heads[head], key_heads[shared].T, preferred_element_type=jnp.float32) * (HD ** -0.5)
            scores = jnp.where(visible, scores, -1e30)
            highest = jnp.max(scores, axis=-1)
            expo = jnp.exp(scores - highest[:, None])
            totals = jnp.sum(expo, axis=-1)
            weights = expo.astype(jnp.bfloat16).astype(jnp.float32)
            summed = jnp.dot(weights, value_heads[shared].astype(jnp.float32), preferred_element_type=jnp.float32)
            return summed / totals[:, None]

        per_head = lax.map(one_head, jnp.arange(H, dtype=jnp.int32))
        attended = per_head.transpose(1, 0, 2).reshape(NEWQ, H * HD)
        keep_rows = jnp.arange(NEWQ, dtype=jnp.int32) < new_count[request]
        attended = jnp.where(keep_rows[:, None], attended, 0.0)
        results.append(attended.astype(jnp.bfloat16))
    return jnp.stack(results, axis=1)
```

```python
import math

import jax, jax.numpy as jnp
from jax import lax
from jax.experimental import pallas as pl
from jax.experimental.pallas import tpu as pltpu
from jax.sharding import PartitionSpec as P

HD = 128
NEWQ = 256
TB = 64
HPT = 4
ROWS = TB * HPT
HIDDEN = -1e30
RATE = math.log2(math.e) * HD ** (-0.5)


def attend_kernel(meta, q_ref, kt_ref, v_ref, o_ref, s0, s1, vx, lse):
    slots = kt_ref.shape[1]
    heads = q_ref.shape[1] // HD
    groups = heads // HPT
    ctx_len, new_count, base = meta[0], meta[1], meta[2]
    lane = lax.broadcasted_iota(jnp.int32, (TB, HD), 1)
    edge = ctx_len - base + 1
    some = edge + NEWQ - 1 > 0
    tiles = jnp.where(some, groups * ((new_count + TB - 1) // TB), 0)

    lse[...] = jnp.full(lse.shape, HIDDEN, jnp.float32)

    @pl.when(tiles < groups * (NEWQ // TB))
    def _():
        o_ref[...] = jnp.zeros(o_ref.shape, o_ref.dtype)

    vx[:, :HD] = v_ref[...]
    vx[:, HD:] = jnp.ones((slots, HD), vx.dtype)

    def place(i):
        row = pl.multiple_of((i // groups) * TB, TB)
        col = pl.multiple_of((i % groups) * (HPT * HD), HPT * HD)
        return row, col

    def scores(i, s):
        row, col = place(i)
        q = jnp.concatenate(
            [q_ref[pl.ds(row, TB), pl.ds(col + h * HD, HD)] for h in range(HPT)], axis=0)
        s[...] = jnp.dot(q, kt_ref[...], preferred_element_type=jnp.float32)

    def hide(i, s):
        row, _ = place(i)
        first = jnp.maximum(edge + row, 0) // HD

        @pl.loop(first, slots // HD)
        def _(c):
            at = pl.multiple_of(c * HD, HD)
            key = lax.broadcasted_iota(jnp.int32, (ROWS, HD), 1) + at
            tok = lax.broadcasted_iota(jnp.int32, (ROWS, HD), 0) % TB
            seen = key < edge + row + tok
            s[:, pl.ds(at, HD)] = jnp.where(seen, s[:, pl.ds(at, HD)], HIDDEN)

    def finish(i, s):
        row, col = place(i)
        top = jnp.max(s[...], axis=1, keepdims=True) * RATE
        p = jnp.exp2(s[...] * RATE - top).astype(jnp.bfloat16)
        acc = jnp.dot(p, vx[...], preferred_element_type=jnp.float32)
        total = acc[:, HD:]
        out = acc[:, :HD] / total
        ls = top + jnp.log2(total)
        kept = lse[pl.ds(row, TB), :]
        for h in range(HPT):
            part = slice(h * TB, (h + 1) * TB)
            o_ref[pl.ds(row, TB), pl.ds(col + h * HD, HD)] = out[part].astype(jnp.bfloat16)
            kept = jnp.where(lane % heads == (i % groups) * HPT + h, ls[part], kept)
        lse[pl.ds(row, TB), :] = kept

    @pl.when(tiles > 0)
    def _():
        scores(0, s0)

        @pl.when(edge < slots)
        def _():
            hide(0, s0)

        @pl.loop(0, tiles // 2)
        def _(j):
            scores(2 * j + 1, s1)
            finish(2 * j, s0)

            @pl.when(edge < slots)
            def _():
                hide(2 * j + 1, s1)

            nxt = jnp.minimum(2 * j + 2, tiles - 1)
            scores(nxt, s0)
            finish(2 * j + 1, s1)

            @pl.when(edge < slots)
            def _():
                hide(nxt, s0)

    full = lse[...]
    lanes = lax.broadcasted_iota(jnp.int32, full.shape, 1)
    high = full.astype(jnp.bfloat16).astype(jnp.float32)
    rest = full - high
    mid = rest.astype(jnp.bfloat16).astype(jnp.float32)
    packed = jnp.where(lanes < heads, high, jnp.where(lanes < 2 * heads, mid, rest - mid))
    o_ref[:, heads * HD:] = packed.astype(jnp.bfloat16)


def attend(meta, q, kt, v):
    rows, width = q.shape
    slots = kt.shape[1]
    heads = width // HD
    return pl.pallas_call(
        attend_kernel,
        out_shape=jax.ShapeDtypeStruct((rows, width + HD), jnp.bfloat16),
        in_specs=[pl.BlockSpec(memory_space=pltpu.SMEM)] + [pl.BlockSpec(memory_space=pltpu.VMEM)] * 3,
        out_specs=pl.BlockSpec(memory_space=pltpu.VMEM),
        scratch_shapes=[
            pltpu.VMEM((ROWS, slots), jnp.float32),
            pltpu.VMEM((ROWS, slots), jnp.float32),
            pltpu.VMEM((slots, 2 * HD), jnp.bfloat16),
            pltpu.VMEM((rows, HD), jnp.float32),
        ],
        compiler_params=pltpu.CompilerParams(vmem_limit_bytes=40 * 2**20),
        cost_estimate=pl.CostEstimate(
            flops=8 * rows * heads * slots * HD, bytes_accessed=4 * 2**20,
            transcendentals=rows * heads * slots),
    )(meta, q, kt, v)


def merge_kernel(meta, part_ref, out_ref, *, cycle, heads):
    srcs, rows = part_ref.shape[0], part_ref.shape[1]
    tps = srcs // cycle
    width = heads * HD
    keep = lax.broadcasted_iota(jnp.int32, (rows, HD), 0) + meta[1] < meta[0]
    for t in range(tps):
        logs = []
        for c in range(cycle):
            packed = part_ref[c * tps + t, :, width:].astype(jnp.float32)
            logs.append(packed[:, :heads] + packed[:, heads:2 * heads] + packed[:, 2 * heads:3 * heads])
        top = logs[0]
        for ls in logs[1:]:
            top = jnp.maximum(top, ls)
        share = [jnp.exp2(ls - top) for ls in logs]
        total = share[0]
        for s in share[1:]:
            total = total + s
        share = [s / total for s in share]
        for h in range(heads):
            at = slice(h * HD, (h + 1) * HD)
            acc = jnp.zeros((rows, HD), jnp.float32)
            for c in range(cycle):
                acc = acc + share[c][:, h:h + 1] * part_ref[c * tps + t, :, at].astype(jnp.float32)
            out_ref[:, pl.ds(t * width + h * HD, HD)] = jnp.where(keep, acc, 0.0)


def merge(meta, parts, cycle, heads):
    srcs, rows, _ = parts.shape
    tps = srcs // cycle
    return pl.pallas_call(
        lambda *refs: merge_kernel(*refs, cycle=cycle, heads=heads),
        out_shape=jax.ShapeDtypeStruct((rows, tps * heads * HD), jnp.float32),
        in_specs=[pl.BlockSpec(memory_space=pltpu.SMEM), pl.BlockSpec(memory_space=pltpu.VMEM)],
        out_specs=pl.BlockSpec(memory_space=pltpu.VMEM),
        compiler_params=pltpu.CompilerParams(vmem_limit_bytes=40 * 2**20),
        cost_estimate=pl.CostEstimate(
            flops=2 * parts.size, bytes_accessed=2 * parts.size, transcendentals=0),
    )(meta, parts)


def shards(queries, key_cache, value_cache, ctx_len, new_count):
    cycle = lax.axis_size("ctx")
    tps = lax.axis_size("tp")
    here = lax.axis_index("ctx")
    rows, reqs, width = queries.shape
    heads = width // HD
    slots = key_cache.shape[0]
    owners = cycle * tps
    tok_rows = NEWQ // owners
    first_row = (here * tps + lax.axis_index("tp")) * tok_rows
    outs = []
    for r in range(reqs):
        q = jnp.broadcast_to(queries[None, :, r], (cycle, rows, width))
        q = lax.all_to_all(q, "ctx", split_axis=0, concat_axis=0).reshape(NEWQ, width)
        meta = jnp.stack([ctx_len[r], new_count[r], here * slots])
        part = attend(meta, q, key_cache[:, r].T, value_cache[:, r])
        part = part.reshape(owners, tok_rows, width + HD)
        part = lax.all_to_all(part, ("ctx", "tp"), split_axis=0, concat_axis=0)
        outs.append(merge(jnp.stack([new_count[r], first_row]), part, cycle, heads))
    return jnp.stack(outs, axis=1).astype(jnp.bfloat16)


def solution(mesh):
    in_specs = (
        P("ctx", "req", "tp"),
        P("ctx", "req", "tp"),
        P("ctx", "req", "tp"),
        P("req"),
        P("req"),
    )
    out_specs = P(("ctx", "tp"), "req", None)
    return jax.shard_map(shards, mesh=mesh, in_specs=in_specs, out_specs=out_specs, check_vma=False)
```

```python
import math

import jax
import jax.numpy as jnp
from jax import lax
from jax.experimental import pallas as pl
from jax.experimental.pallas import tpu as pltpu
from jax.sharding import PartitionSpec as P

HD = 128
NEWQ = 256
TB = 32
KC = 256
HIDDEN = -1e30
RATE = math.log2(math.e) * HD ** (-0.5)
VMEM = pl.BlockSpec(memory_space=pltpu.VMEM)
SMEM = pl.BlockSpec(memory_space=pltpu.SMEM)


def pack_logs(ls, heads):
    lanes = lax.broadcasted_iota(jnp.int32, ls.shape, 1)
    high = ls.astype(jnp.bfloat16).astype(jnp.float32)
    rest = ls - high
    mid = rest.astype(jnp.bfloat16).astype(jnp.float32)
    packed = jnp.where(lanes < heads, high, jnp.where(lanes < 2 * heads, mid, rest - mid))
    return packed.astype(jnp.bfloat16)


def attend_kernel(meta, q_ref, k_ref, vt_ref, o_ref, s0, s1, mx0, mx1):
    slots = k_ref.shape[0]
    width = q_ref.shape[1]
    heads = width // HD
    lanes = heads * TB
    ctx_len, new_count, base = meta[0], meta[1], meta[2]
    edge = ctx_len - base + 1
    some = edge + NEWQ - 1 > 0
    tiles = jnp.where(some, (new_count + TB - 1) // TB, 0)
    of_head = lax.broadcasted_iota(jnp.int32, (TB, HD), 1) % heads
    token = lax.broadcasted_iota(jnp.int32, (KC, lanes), 1) % TB
    ahead = lax.broadcasted_iota(jnp.int32, (KC, lanes), 0) - token

    @pl.loop(tiles, NEWQ // TB)
    def _(i):
        row = pl.multiple_of(i * TB, TB)
        o_ref[pl.ds(row, TB), :width] = jnp.zeros((TB, width), o_ref.dtype)
        o_ref[pl.ds(row, TB), width:] = pack_logs(jnp.full((TB, HD), HIDDEN, jnp.float32), heads)

    def step(i, s, mx, done, s_done, mx_done, span, clear):
        row = pl.multiple_of(i * TB, TB)
        q = jnp.concatenate(
            [q_ref[pl.ds(row, TB), h * HD:(h + 1) * HD] for h in range(heads)], axis=0)
        if done is not None:
            shift = jnp.max(mx_done[...], axis=0, keepdims=True) * RATE
        top = acc = total = None
        for c in range(span):
            at = slice(c * KC, (c + 1) * KC)
            part = lax.dot_general(k_ref[at, :], q, (((1,), (1,)), ((), ())),
                                   preferred_element_type=jnp.float32)
            if c >= clear:
                part = jnp.where(ahead < edge + row - c * KC, part, HIDDEN)
            s[at, :] = part
            high = jnp.max(part.reshape(KC // 8, 8, lanes), axis=0)
            top = high if top is None else jnp.maximum(top, high)
            if done is not None:
                e = jnp.exp2(s_done[at, :] * RATE - shift)
                add = jnp.sum(e.reshape(KC // 8, 8, lanes), axis=0)
                total = add if total is None else total + add
                new = jnp.dot(vt_ref[:, at], e.astype(jnp.bfloat16),
                              preferred_element_type=jnp.float32)
                acc = new if acc is None else acc + new
        mx[...] = top
        if done is None:
            return
        row = pl.multiple_of(done * TB, TB)
        total = jnp.sum(total, axis=0, keepdims=True)
        out = (acc / total).T
        ls = jnp.broadcast_to(shift + jnp.log2(total), (HD, lanes)).T
        kept = jnp.zeros((TB, HD), jnp.float32)
        for h in range(heads):
            at = slice(h * TB, (h + 1) * TB)
            o_ref[pl.ds(row, TB), h * HD:(h + 1) * HD] = out[at].astype(o_ref.dtype)
            kept = jnp.where(of_head == h, ls[at], kept)
        o_ref[pl.ds(row, TB), width:] = pack_logs(kept, heads)

    def run(span, clear):
        step(0, s0, mx0, None, None, None, span, clear)
        last = tiles - 1

        @pl.loop(0, (tiles + 1) // 2)
        def _(j):
            step(jnp.minimum(2 * j + 1, last), s1, mx1, 2 * j, s0, mx0, span, clear)
            done = jnp.minimum(2 * j + 1, last)
            step(jnp.minimum(2 * j + 2, last), s0, mx0, done, s1, mx1, span, clear)

    chunks = slots // KC
    half = chunks // 2
    near = (half + 1) * KC - (NEWQ - 1)
    for low, high, span, clear in (
        (slots, None, chunks, chunks),
        (slots - KC, slots, chunks, chunks - 1),
        (near, slots - KC, chunks, half),
        (None, near, half + 1, 0),
    ):
        here = tiles > 0
        if low is not None:
            here = here & (edge >= low)
        if high is not None:
            here = here & (edge < high)

        @pl.when(here)
        def _(span=span, clear=clear):
            run(span, clear)


def attend(meta, q, k, vt):
    rows, width = q.shape
    slots = k.shape[0]
    heads = width // HD
    return pl.pallas_call(
        attend_kernel,
        out_shape=jax.ShapeDtypeStruct((rows, width + HD), jnp.bfloat16),
        in_specs=[SMEM, VMEM, VMEM, VMEM],
        out_specs=VMEM,
        scratch_shapes=[
            pltpu.VMEM((slots, heads * TB), jnp.float32),
            pltpu.VMEM((slots, heads * TB), jnp.float32),
            pltpu.VMEM((8, heads * TB), jnp.float32),
            pltpu.VMEM((8, heads * TB), jnp.float32),
        ],
        compiler_params=pltpu.CompilerParams(vmem_limit_bytes=40 * 2**20),
        cost_estimate=pl.CostEstimate(
            flops=8 * rows * heads * slots * HD, bytes_accessed=4 * 2**20,
            transcendentals=rows * heads * slots),
    )(meta, q, k, vt)


def part_kernel(k_ref, v_ref, *refs):
    reqs = (len(refs) - 1) // 2
    scratch = refs[-1]
    n = k_ref.shape[0] // reqs
    scratch[0] = k_ref[...].astype(jnp.float32)
    scratch[1] = v_ref[...].astype(jnp.float32)
    for r in range(reqs):
        refs[r][...] = scratch[0, pl.ds(r, n, stride=reqs), :].astype(jnp.bfloat16)
        refs[reqs + r][...] = scratch[1, pl.ds(r, n, stride=reqs), :].T.astype(jnp.bfloat16)


def part_caches(keys, values):
    slots, reqs, _ = keys.shape
    n = 512
    flat = pl.BlockSpec((n * reqs, HD), lambda i: (i, 0))
    shape = jax.ShapeDtypeStruct((slots, HD), jnp.bfloat16)
    turned = jax.ShapeDtypeStruct((HD, slots), jnp.bfloat16)
    outs = pl.pallas_call(
        part_kernel,
        grid=(slots // n,),
        out_shape=[shape] * reqs + [turned] * reqs,
        in_specs=[flat, flat],
        out_specs=[pl.BlockSpec((n, HD), lambda i: (i, 0))] * reqs
        + [pl.BlockSpec((HD, n), lambda i: (0, i))] * reqs,
        scratch_shapes=[pltpu.VMEM((2, n * reqs, HD), jnp.float32)],
        compiler_params=pltpu.CompilerParams(vmem_limit_bytes=16 * 2**20),
        cost_estimate=pl.CostEstimate(
            flops=0, bytes_accessed=8 * keys.size, transcendentals=0),
    )(keys.reshape(slots * reqs, HD), values.reshape(slots * reqs, HD))
    return outs[:reqs], outs[reqs:]


def merge_kernel(meta, part_ref, out_ref, *, cycle, heads):
    srcs, rows = part_ref.shape[0], part_ref.shape[1]
    tps = srcs // cycle
    width = heads * HD
    keep = lax.broadcasted_iota(jnp.int32, (rows, HD), 0) + meta[1] < meta[0]
    for t in range(tps):
        logs = []
        for c in range(cycle):
            packed = part_ref[c * tps + t, :, width:].astype(jnp.float32)
            logs.append(packed[:, :heads] + packed[:, heads:2 * heads] + packed[:, 2 * heads:3 * heads])
        top = logs[0]
        for ls in logs[1:]:
            top = jnp.maximum(top, ls)
        share = [jnp.exp2(ls - top) for ls in logs]
        total = share[0]
        for s in share[1:]:
            total = total + s
        share = [s / total for s in share]
        for h in range(heads):
            at = slice(h * HD, (h + 1) * HD)
            acc = jnp.zeros((rows, HD), jnp.float32)
            for c in range(cycle):
                acc = acc + share[c][:, h:h + 1] * part_ref[c * tps + t, :, at].astype(jnp.float32)
            out_ref[:, pl.ds(t * width + h * HD, HD)] = jnp.where(keep, acc, 0.0)


def merge(meta, parts, cycle, heads):
    srcs, rows, _ = parts.shape
    tps = srcs // cycle
    return pl.pallas_call(
        lambda *refs: merge_kernel(*refs, cycle=cycle, heads=heads),
        out_shape=jax.ShapeDtypeStruct((rows, tps * heads * HD), jnp.float32),
        in_specs=[pl.BlockSpec(memory_space=pltpu.SMEM), pl.BlockSpec(memory_space=pltpu.VMEM)],
        out_specs=pl.BlockSpec(memory_space=pltpu.VMEM),
        compiler_params=pltpu.CompilerParams(vmem_limit_bytes=40 * 2**20),
        cost_estimate=pl.CostEstimate(
            flops=2 * parts.size, bytes_accessed=2 * parts.size, transcendentals=0),
    )(meta, parts)


def shards(queries, key_cache, value_cache, ctx_len, new_count):
    cycle = lax.axis_size("ctx")
    tps = lax.axis_size("tp")
    here = lax.axis_index("ctx")
    rows, reqs, width = queries.shape
    heads = width // HD
    slots = key_cache.shape[0]
    owners = cycle * tps
    tok_rows = NEWQ // owners
    first_row = (here * tps + lax.axis_index("tp")) * tok_rows
    outs = []
    keys, turned = part_caches(key_cache, value_cache)
    for r in range(reqs):
        q = jnp.broadcast_to(queries[None, :, r], (cycle, rows, width))
        q = lax.all_to_all(q, "ctx", split_axis=0, concat_axis=0).reshape(NEWQ, width)
        part = attend(jnp.stack([ctx_len[r], new_count[r], here * slots]), q, keys[r], turned[r])
        part = part.reshape(owners, tok_rows, width + HD)
        part = lax.all_to_all(part, ("ctx", "tp"), split_axis=0, concat_axis=0)
        outs.append(merge(jnp.stack([new_count[r], first_row]), part, cycle, heads))
    return jnp.stack(outs, axis=1).astype(jnp.bfloat16)


def solution(mesh):
    in_specs = (
        P("ctx", "req", "tp"),
        P("ctx", "req", "tp"),
        P("ctx", "req", "tp"),
        P("req"),
        P("req"),
    )
    out_specs = P(("ctx", "tp"), "req", None)
    return jax.shard_map(shards, mesh=mesh, in_specs=in_specs, out_specs=out_specs, check_vma=False)
```

```python
import math

import jax
import jax.numpy as jnp
from jax import lax
from jax.experimental import pallas as pl
from jax.experimental.pallas import tpu as pltpu
from jax.sharding import PartitionSpec as P

HD = 128
NEWQ = 256
TB = 32
KC = 256
HIDDEN = -1e30
RATE = math.log2(math.e) * HD ** (-0.5)
VMEM = pl.BlockSpec(memory_space=pltpu.VMEM)
SMEM = pl.BlockSpec(memory_space=pltpu.SMEM)


def pack_logs(ls, heads):
    lanes = lax.broadcasted_iota(jnp.int32, ls.shape, 1)
    high = ls.astype(jnp.bfloat16).astype(jnp.float32)
    rest = ls - high
    mid = rest.astype(jnp.bfloat16).astype(jnp.float32)
    packed = jnp.where(lanes < heads, high, jnp.where(lanes < 2 * heads, mid, rest - mid))
    return packed.astype(jnp.bfloat16)


def attend_kernel(meta, q_ref, k_ref, vt_ref, o_ref, s, mx):
    slots = k_ref.shape[0]
    width = q_ref.shape[1]
    heads = width // HD
    lanes = heads * TB
    ctx_len, new_count, base = meta[0], meta[1], meta[2]
    edge = ctx_len - base + 1
    some = edge + NEWQ - 1 > 0
    tiles = jnp.where(some, (new_count + TB - 1) // TB, 0)
    of_head = lax.broadcasted_iota(jnp.int32, (TB, HD), 1) % heads
    token = lax.broadcasted_iota(jnp.int32, (1, lanes), 1) % TB
    key = lax.broadcasted_iota(jnp.int32, (KC, lanes), 0)

    @pl.loop(tiles, NEWQ // TB)
    def _(i):
        row = pl.multiple_of(i * TB, TB)
        o_ref[pl.ds(row, TB), :width] = jnp.zeros((TB, width), o_ref.dtype)
        o_ref[pl.ds(row, TB), width:] = pack_logs(jnp.full((TB, HD), HIDDEN, jnp.float32), heads)

    def step(i, span, clear):
        row = pl.multiple_of(jnp.minimum(i, tiles - 1) * TB, TB)
        q = jnp.concatenate(
            [q_ref[pl.ds(row, TB), h * HD:(h + 1) * HD] for h in range(heads)], axis=0)
        shown = edge + row + token
        shift = jnp.max(mx[...], axis=0, keepdims=True) * RATE
        top = acc = total = None
        for c in range(span):
            at = slice(c * KC, (c + 1) * KC)
            e = jnp.exp2(s[at, :] * RATE - shift)
            part = lax.dot_general(k_ref[at, :], q, (((1,), (1,)), ((), ())),
                                   preferred_element_type=jnp.float32)
            if c >= clear:
                part = jnp.where(key < shown - c * KC, part, HIDDEN)
            s[at, :] = part
            high = jnp.max(part.reshape(KC // 8, 8, lanes), axis=0)
            top = high if top is None else jnp.maximum(top, high)
            add = jnp.sum(e.reshape(KC // 8, 8, lanes), axis=0)
            total = add if total is None else total + add
            new = jnp.dot(vt_ref[:, at], e.astype(jnp.bfloat16), preferred_element_type=jnp.float32)
            acc = new if acc is None else acc + new
        mx[...] = top
        row = pl.multiple_of(jnp.maximum(i - 1, 0) * TB, TB)
        total = jnp.sum(total, axis=0, keepdims=True)
        out = (acc / total).T
        ls = jnp.broadcast_to(shift + jnp.log2(total), (HD, lanes)).T
        kept = jnp.zeros((TB, HD), jnp.float32)
        for h in range(heads):
            at = slice(h * TB, (h + 1) * TB)
            o_ref[pl.ds(row, TB), h * HD:(h + 1) * HD] = out[at].astype(o_ref.dtype)
            kept = jnp.where(of_head == h, ls[at], kept)
        o_ref[pl.ds(row, TB), width:] = pack_logs(kept, heads)

    def run(span, clear):
        @pl.loop(0, tiles + 1)
        def _(i):
            step(i, span, clear)

    chunks = slots // KC
    cuts = (0, 3, 7, 10, chunks - 1, chunks)
    for low, high in zip(cuts, cuts[1:] + (None,)):
        span = chunks if high is None else min(chunks, high + NEWQ // KC)
        clear = low
        here = tiles > 0
        if low > 0:
            here = here & (edge >= low * KC)
        if high is not None:
            here = here & (edge < high * KC)

        @pl.when(here)
        def _(span=span, clear=clear):
            run(span, clear)


def attend(meta, q, k, vt):
    rows, width = q.shape
    slots = k.shape[0]
    heads = width // HD
    return pl.pallas_call(
        attend_kernel,
        out_shape=jax.ShapeDtypeStruct((rows, width + HD), jnp.bfloat16),
        in_specs=[SMEM, VMEM, VMEM, VMEM],
        out_specs=VMEM,
        scratch_shapes=[
            pltpu.VMEM((slots, heads * TB), jnp.float32),
            pltpu.VMEM((8, heads * TB), jnp.float32),
        ],
        compiler_params=pltpu.CompilerParams(vmem_limit_bytes=40 * 2**20),
        cost_estimate=pl.CostEstimate(
            flops=8 * rows * heads * slots * HD, bytes_accessed=4 * 2**20,
            transcendentals=rows * heads * slots),
    )(meta, q, k, vt)


def part_kernel(k_ref, v_ref, *refs):
    reqs = (len(refs) - 1) // 2
    scratch = refs[-1]
    n = k_ref.shape[0] // reqs
    scratch[0] = k_ref[...].astype(jnp.float32)
    scratch[1] = v_ref[...].astype(jnp.float32)
    for r in range(reqs):
        refs[r][...] = scratch[0, pl.ds(r, n, stride=reqs), :].astype(jnp.bfloat16)
        refs[reqs + r][...] = scratch[1, pl.ds(r, n, stride=reqs), :].T.astype(jnp.bfloat16)


def part_caches(keys, values):
    slots, reqs, _ = keys.shape
    n = 512
    flat = pl.BlockSpec((n * reqs, HD), lambda i: (i, 0))
    shape = jax.ShapeDtypeStruct((slots, HD), jnp.bfloat16)
    turned = jax.ShapeDtypeStruct((HD, slots), jnp.bfloat16)
    outs = pl.pallas_call(
        part_kernel,
        grid=(slots // n,),
        out_shape=[shape] * reqs + [turned] * reqs,
        in_specs=[flat, flat],
        out_specs=[pl.BlockSpec((n, HD), lambda i: (i, 0))] * reqs
        + [pl.BlockSpec((HD, n), lambda i: (0, i))] * reqs,
        scratch_shapes=[pltpu.VMEM((2, n * reqs, HD), jnp.float32)],
        compiler_params=pltpu.CompilerParams(vmem_limit_bytes=16 * 2**20),
        cost_estimate=pl.CostEstimate(
            flops=0, bytes_accessed=8 * keys.size, transcendentals=0),
    )(keys.reshape(slots * reqs, HD), values.reshape(slots * reqs, HD))
    return outs[:reqs], outs[reqs:]


def merge_kernel(meta, part_ref, out_ref, *, cycle, heads):
    srcs, rows = part_ref.shape[0], part_ref.shape[1]
    tps = srcs // cycle
    width = heads * HD
    keep = lax.broadcasted_iota(jnp.int32, (rows, HD), 0) + meta[1] < meta[0]
    for t in range(tps):
        logs = []
        for c in range(cycle):
            packed = part_ref[c * tps + t, :, width:].astype(jnp.float32)
            logs.append(packed[:, :heads] + packed[:, heads:2 * heads] + packed[:, 2 * heads:3 * heads])
        top = logs[0]
        for ls in logs[1:]:
            top = jnp.maximum(top, ls)
        share = [jnp.exp2(ls - top) for ls in logs]
        total = share[0]
        for s in share[1:]:
            total = total + s
        share = [s / total for s in share]
        for h in range(heads):
            at = slice(h * HD, (h + 1) * HD)
            acc = jnp.zeros((rows, HD), jnp.float32)
            for c in range(cycle):
                acc = acc + share[c][:, h:h + 1] * part_ref[c * tps + t, :, at].astype(jnp.float32)
            out_ref[:, pl.ds(t * width + h * HD, HD)] = jnp.where(keep, acc, 0.0)


def merge(meta, parts, cycle, heads):
    srcs, rows, _ = parts.shape
    tps = srcs // cycle
    return pl.pallas_call(
        lambda *refs: merge_kernel(*refs, cycle=cycle, heads=heads),
        out_shape=jax.ShapeDtypeStruct((rows, tps * heads * HD), jnp.float32),
        in_specs=[pl.BlockSpec(memory_space=pltpu.SMEM), pl.BlockSpec(memory_space=pltpu.VMEM)],
        out_specs=pl.BlockSpec(memory_space=pltpu.VMEM),
        compiler_params=pltpu.CompilerParams(vmem_limit_bytes=40 * 2**20),
        cost_estimate=pl.CostEstimate(
            flops=2 * parts.size, bytes_accessed=2 * parts.size, transcendentals=0),
    )(meta, parts)


def shards(queries, key_cache, value_cache, ctx_len, new_count):
    cycle = lax.axis_size("ctx")
    tps = lax.axis_size("tp")
    here = lax.axis_index("ctx")
    rows, reqs, width = queries.shape
    heads = width // HD
    slots = key_cache.shape[0]
    owners = cycle * tps
    tok_rows = NEWQ // owners
    first_row = (here * tps + lax.axis_index("tp")) * tok_rows
    outs = []
    keys, turned = part_caches(key_cache, value_cache)
    for r in range(reqs):
        q = jnp.broadcast_to(queries[None, :, r], (cycle, rows, width))
        q = lax.all_to_all(q, "ctx", split_axis=0, concat_axis=0).reshape(NEWQ, width)
        part = attend(jnp.stack([ctx_len[r], new_count[r], here * slots]), q, keys[r], turned[r])
        part = part.reshape(owners, tok_rows, width + HD)
        part = lax.all_to_all(part, ("ctx", "tp"), split_axis=0, concat_axis=0)
        outs.append(merge(jnp.stack([new_count[r], first_row]), part, cycle, heads))
    return jnp.stack(outs, axis=1).astype(jnp.bfloat16)


def solution(mesh):
    in_specs = (
        P("ctx", "req", "tp"),
        P("ctx", "req", "tp"),
        P("ctx", "req", "tp"),
        P("req"),
        P("req"),
    )
    out_specs = P(("ctx", "tp"), "req", None)
    return jax.shard_map(shards, mesh=mesh, in_specs=in_specs, out_specs=out_specs, check_vma=False)
```

```python
import functools
import math

import jax
import jax.numpy as jnp
from jax import lax
from jax.experimental import pallas as pl
from jax.experimental.pallas import tpu as pltpu
from jax.sharding import PartitionSpec as P

HD = 128
NEWQ = 256
TB = 32
KC = 256
HIDDEN = -1e30
RATE = math.log2(math.e) * HD ** (-0.5)
VMEM = pl.BlockSpec(memory_space=pltpu.VMEM)
SMEM = pl.BlockSpec(memory_space=pltpu.SMEM)


def pack_logs(ls, heads):
    lanes = lax.broadcasted_iota(jnp.int32, ls.shape, 1)
    high = ls.astype(jnp.bfloat16).astype(jnp.float32)
    rest = ls - high
    mid = rest.astype(jnp.bfloat16).astype(jnp.float32)
    packed = jnp.where(lanes < heads, high, jnp.where(lanes < 2 * heads, mid, rest - mid))
    return packed.astype(jnp.bfloat16)


def attend_kernel(req, meta, *refs):
    *q_refs, k_ref, vt_ref, o_ref, s, mx, q_all = refs
    slots = k_ref.shape[0]
    width = k_ref.shape[1] * ((o_ref.shape[1] - HD) // HD)
    heads = width // HD
    lanes = heads * TB
    reqs = (meta.shape[0] - 4) // 2
    ctx_len, new_count, base = meta[req], meta[reqs + req], meta[2 * reqs]
    edge = ctx_len - base + 1
    some = edge + NEWQ - 1 > 0
    tiles = jnp.where(some, (new_count + TB - 1) // TB, 0)
    q_ref = q_refs[0]
    if len(q_refs) > 1:
        ring = len(q_refs)
        q_ref = q_all
        for n, pair in enumerate(q_refs):
            for m in range(2):
                block = (meta[2 * reqs + 1] + m) % 2 * ring + (meta[2 * reqs + 2] - n + ring) % ring
                q_all[pl.ds(pl.multiple_of(block * TB, TB), TB), :] = pair[m * TB:(m + 1) * TB, :]
    of_head = lax.broadcasted_iota(jnp.int32, (TB, HD), 1) % heads
    token = lax.broadcasted_iota(jnp.int32, (1, lanes), 1) % TB
    key = lax.broadcasted_iota(jnp.int32, (KC, lanes), 0)

    @pl.loop(tiles, NEWQ // TB)
    def _(i):
        row = pl.multiple_of(i * TB, TB)
        o_ref[pl.ds(row, TB), :width] = jnp.zeros((TB, width), o_ref.dtype)
        o_ref[pl.ds(row, TB), width:] = pack_logs(jnp.full((TB, HD), HIDDEN, jnp.float32), heads)

    def step(i, span, clear):
        row = pl.multiple_of(jnp.minimum(i, tiles - 1) * TB, TB)
        q = jnp.concatenate(
            [q_ref[pl.ds(row, TB), h * HD:(h + 1) * HD] for h in range(heads)], axis=0)
        shown = edge + row + token
        shift = jnp.max(mx[...], axis=0, keepdims=True) * RATE
        top = acc = total = None
        for c in range(span):
            at = slice(c * KC, (c + 1) * KC)
            e = jnp.exp2(s[at, :] * RATE - shift)
            part = lax.dot_general(k_ref[at, :], q, (((1,), (1,)), ((), ())),
                                   preferred_element_type=jnp.float32)
            if c >= clear:
                part = jnp.where(key < shown - c * KC, part, HIDDEN)
            s[at, :] = part
            high = jnp.max(part.reshape(KC // 8, 8, lanes), axis=0)
            top = high if top is None else jnp.maximum(top, high)
            add = jnp.sum(e.reshape(KC // 8, 8, lanes), axis=0)
            total = add if total is None else total + add
            new = jnp.dot(vt_ref[:, at], e.astype(jnp.bfloat16), preferred_element_type=jnp.float32)
            acc = new if acc is None else acc + new
        mx[...] = top
        row = pl.multiple_of(jnp.maximum(i - 1, 0) * TB, TB)
        total = jnp.sum(total, axis=0, keepdims=True)
        out = (acc / total).T
        ls = jnp.broadcast_to(shift + jnp.log2(total), (HD, lanes)).T
        kept = jnp.zeros((TB, HD), jnp.float32)
        for h in range(heads):
            at = slice(h * TB, (h + 1) * TB)
            o_ref[pl.ds(row, TB), h * HD:(h + 1) * HD] = out[at].astype(o_ref.dtype)
            kept = jnp.where(of_head == h, ls[at], kept)
        o_ref[pl.ds(row, TB), width:] = pack_logs(kept, heads)

    def run(span, clear):
        @pl.loop(0, tiles + 1)
        def _(i):
            step(i, span, clear)

    chunks = slots // KC
    cuts = (0, 3, 7, 10, chunks - 1, chunks)
    for low, high in zip(cuts, cuts[1:] + (None,)):
        span = chunks if high is None else min(chunks, high + NEWQ // KC)
        clear = low
        here = tiles > 0
        if low > 0:
            here = here & (edge >= low * KC)
        if high is not None:
            here = here & (edge < high * KC)

        @pl.when(here)
        def _(span=span, clear=clear):
            run(span, clear)


def attend(req, meta, qs, k, vt):
    rows, width = NEWQ, qs[0].shape[1]
    slots = k.shape[0]
    heads = width // HD
    return pl.pallas_call(
        functools.partial(attend_kernel, req),
        out_shape=jax.ShapeDtypeStruct((rows, width + HD), jnp.bfloat16),
        in_specs=[SMEM] + [VMEM] * (len(qs) + 2),
        out_specs=VMEM,
        scratch_shapes=[
            pltpu.VMEM((slots, heads * TB), jnp.float32),
            pltpu.VMEM((8, heads * TB), jnp.float32),
            pltpu.VMEM((rows if len(qs) > 1 else TB, width), jnp.bfloat16),
        ],
        compiler_params=pltpu.CompilerParams(vmem_limit_bytes=40 * 2**20),
        cost_estimate=pl.CostEstimate(
            flops=8 * rows * heads * slots * HD, bytes_accessed=4 * 2**20,
            transcendentals=rows * heads * slots),
    )(meta, *qs, k, vt)


def part_kernel(k_ref, v_ref, *refs):
    reqs = (len(refs) - 1) // 2
    scratch = refs[-1]
    n = k_ref.shape[0] // reqs
    scratch[0] = k_ref[...].astype(jnp.float32)
    scratch[1] = v_ref[...].astype(jnp.float32)
    for r in range(reqs):
        refs[r][...] = scratch[0, pl.ds(r, n, stride=reqs), :].astype(jnp.bfloat16)
        refs[reqs + r][...] = scratch[1, pl.ds(r, n, stride=reqs), :].T.astype(jnp.bfloat16)


def part_caches(keys, values):
    slots, reqs, _ = keys.shape
    n = 512
    flat = pl.BlockSpec((n * reqs, HD), lambda i: (i, 0))
    shape = jax.ShapeDtypeStruct((slots, HD), jnp.bfloat16)
    turned = jax.ShapeDtypeStruct((HD, slots), jnp.bfloat16)
    outs = pl.pallas_call(
        part_kernel,
        grid=(slots // n,),
        out_shape=[shape] * reqs + [turned] * reqs,
        in_specs=[flat, flat],
        out_specs=[pl.BlockSpec((n, HD), lambda i: (i, 0))] * reqs
        + [pl.BlockSpec((HD, n), lambda i: (0, i))] * reqs,
        scratch_shapes=[pltpu.VMEM((2, n * reqs, HD), jnp.float32)],
        compiler_params=pltpu.CompilerParams(vmem_limit_bytes=16 * 2**20),
        cost_estimate=pl.CostEstimate(
            flops=0, bytes_accessed=8 * keys.size, transcendentals=0),
    )(keys.reshape(slots * reqs, HD), values.reshape(slots * reqs, HD))
    return outs[:reqs], outs[reqs:]


def merge_kernel(req, meta, part_ref, out_ref, *, cycle, heads):
    srcs, rows = part_ref.shape[0], part_ref.shape[1]
    tps = srcs // cycle
    width = heads * HD
    keep = lax.broadcasted_iota(jnp.int32, (rows, HD), 0) + meta[meta.shape[0] - 1] < meta[(meta.shape[0] - 4) // 2 + req]
    for t in range(tps):
        logs = []
        for c in range(cycle):
            packed = part_ref[c * tps + t, :, width:].astype(jnp.float32)
            logs.append(packed[:, :heads] + packed[:, heads:2 * heads] + packed[:, 2 * heads:3 * heads])
        top = logs[0]
        for ls in logs[1:]:
            top = jnp.maximum(top, ls)
        share = [jnp.exp2(ls - top) for ls in logs]
        total = share[0]
        for s in share[1:]:
            total = total + s
        share = [s / total for s in share]
        for h in range(heads):
            at = slice(h * HD, (h + 1) * HD)
            acc = jnp.zeros((rows, HD), jnp.float32)
            for c in range(cycle):
                acc = acc + share[c][:, h:h + 1] * part_ref[c * tps + t, :, at].astype(jnp.float32)
            out_ref[:, pl.ds(t * width + h * HD, HD)] = jnp.where(keep, acc, 0.0)


def merge(req, meta, parts, cycle, heads):
    srcs, rows, _ = parts.shape
    tps = srcs // cycle
    return pl.pallas_call(
        functools.partial(merge_kernel, req, cycle=cycle, heads=heads),
        out_shape=jax.ShapeDtypeStruct((rows, tps * heads * HD), jnp.float32),
        in_specs=[pl.BlockSpec(memory_space=pltpu.SMEM), pl.BlockSpec(memory_space=pltpu.VMEM)],
        out_specs=pl.BlockSpec(memory_space=pltpu.VMEM),
        compiler_params=pltpu.CompilerParams(vmem_limit_bytes=40 * 2**20),
        cost_estimate=pl.CostEstimate(
            flops=2 * parts.size, bytes_accessed=2 * parts.size, transcendentals=0),
    )(meta, parts)


def shifted(block, across, along):
    size = lax.axis_size("ctx")
    ring = size // 2
    route = [
        (i, (i // ring + across) % 2 * ring + (i % ring + along) % ring) for i in range(size)
    ]
    return lax.ppermute(block, "ctx", route)


def shards(queries, key_cache, value_cache, ctx_len, new_count):
    cycle = lax.axis_size("ctx")
    tps = lax.axis_size("tp")
    here = lax.axis_index("ctx")
    rows, reqs, width = queries.shape
    heads = width // HD
    slots = key_cache.shape[0]
    owners = cycle * tps
    tok_rows = NEWQ // owners
    first_row = (here * tps + lax.axis_index("tp")) * tok_rows
    ring = cycle // 2
    places = jnp.stack([here * slots, here // ring, here % ring, first_row])
    meta = jnp.concatenate([ctx_len, new_count, places])
    split = queries.transpose(1, 0, 2)
    caches = part_caches(key_cache, value_cache)
    other, meta, (keys, turned) = lax.optimization_barrier((shifted(split, 1, 0), meta, caches))
    pairs = jnp.concatenate([split, other], axis=1)
    outs = []
    for r in range(reqs):
        qs = [pairs[r]] + [shifted(pairs[r], 0, n) for n in range(1, ring)]
        part = attend(r, meta, qs, keys[r], turned[r])
        part = part.reshape(owners, tok_rows, width + HD)
        part = lax.all_to_all(part, ("ctx", "tp"), split_axis=0, concat_axis=0)
        outs.append(merge(r, meta, part, cycle, heads))
    return jnp.stack(outs, axis=1).astype(jnp.bfloat16)


def solution(mesh):
    in_specs = (
        P("ctx", "req", "tp"),
        P("ctx", "req", "tp"),
        P("ctx", "req", "tp"),
        P("req"),
        P("req"),
    )
    out_specs = P(("ctx", "tp"), "req", None)
    return jax.shard_map(shards, mesh=mesh, in_specs=in_specs, out_specs=out_specs, check_vma=False)
```

```python
import functools
import math

import jax
import jax.numpy as jnp
from jax import lax
from jax.experimental import pallas as pl
from jax.experimental.pallas import tpu as pltpu
from jax.sharding import PartitionSpec as P

HD = 128
NEWQ = 256
TB = 32
KC = 256
HIDDEN = -1e30
RATE = math.log2(math.e) * HD ** (-0.5)
VMEM = pl.BlockSpec(memory_space=pltpu.VMEM)
SMEM = pl.BlockSpec(memory_space=pltpu.SMEM)


def pack_logs(ls, heads):
    lanes = lax.broadcasted_iota(jnp.int32, ls.shape, 1)
    high = ls.astype(jnp.bfloat16).astype(jnp.float32)
    rest = ls - high
    mid = rest.astype(jnp.bfloat16).astype(jnp.float32)
    packed = jnp.where(lanes < heads, high, jnp.where(lanes < 2 * heads, mid, rest - mid))
    return packed.astype(jnp.bfloat16)


def sweep(req, place, lead, meta, q_ref, k_ref, vt_ref, o_ref, s, mx, order):
    slots = k_ref.shape[1]
    width = q_ref.shape[2]
    heads = width // HD
    lanes = heads * TB
    count = q_ref.shape[1] // TB
    reqs = (meta.shape[0] - 4) // 2
    ring = NEWQ // TB // 2
    ctx_len, new_count, base = meta[req], meta[reqs + req], meta[2 * reqs]
    edge = ctx_len - base + 1
    some = edge + NEWQ - 1 > 0
    of_head = lax.broadcasted_iota(jnp.int32, (TB, HD), 1) % heads
    token = lax.broadcasted_iota(jnp.int32, (1, lanes), 1) % TB
    key = lax.broadcasted_iota(jnp.int32, (KC, lanes), 0)

    def block(j):
        across, along = lax.rem(j, 2), lead + j // 2
        return (meta[2 * reqs + 1] + across) % 2 * ring + (meta[2 * reqs + 2] - along + ring) % ring

    def spot(j):
        return pl.ds(pl.multiple_of((block(j) if lead else j) * TB, TB), TB)

    def note(j, tiles):
        take = some & (block(j) * TB < new_count)

        @pl.when(take)
        def _():
            order[tiles] = j

        @pl.when(jnp.logical_not(take))
        def _():
            none = jnp.full((TB, HD), HIDDEN, jnp.float32)
            o_ref[place, spot(j), :width] = jnp.zeros((TB, width), o_ref.dtype)
            o_ref[place, spot(j), width:] = pack_logs(none, heads)

        return tiles + take.astype(jnp.int32)

    tiles = lax.fori_loop(0, count, note, jnp.int32(0))

    def step(i, span, clear):
        tile = order[jnp.minimum(i, tiles - 1)]
        row = pl.multiple_of(tile * TB, TB)
        q = jnp.concatenate(
            [q_ref[place, pl.ds(row, TB), h * HD:(h + 1) * HD] for h in range(heads)], axis=0)
        shown = edge + block(tile) * TB + token
        shift = jnp.max(mx[...], axis=0, keepdims=True) * RATE
        top = acc = total = None
        for c in range(span):
            at = slice(c * KC, (c + 1) * KC)
            e = jnp.exp2(s[at, :] * RATE - shift)
            part = lax.dot_general(k_ref[req, at, :], q, (((1,), (1,)), ((), ())),
                                   preferred_element_type=jnp.float32)
            if c >= clear:
                part = jnp.where(key < shown - c * KC, part, HIDDEN)
            s[at, :] = part
            high = jnp.max(part.reshape(KC // 8, 8, lanes), axis=0)
            top = high if top is None else jnp.maximum(top, high)
            add = jnp.sum(e.reshape(KC // 8, 8, lanes), axis=0)
            total = add if total is None else total + add
            new = jnp.dot(vt_ref[req, :, at], e.astype(jnp.bfloat16), preferred_element_type=jnp.float32)
            acc = new if acc is None else acc + new
        mx[...] = top
        there = spot(order[jnp.maximum(i - 1, 0)])
        total = jnp.sum(total, axis=0, keepdims=True)
        out = (acc / total).T
        ls = jnp.broadcast_to(shift + jnp.log2(total), (HD, lanes)).T
        kept = jnp.zeros((TB, HD), jnp.float32)
        for h in range(heads):
            at = slice(h * TB, (h + 1) * TB)
            o_ref[place, there, h * HD:(h + 1) * HD] = out[at].astype(o_ref.dtype)
            kept = jnp.where(of_head == h, ls[at], kept)
        o_ref[place, there, width:] = pack_logs(kept, heads)

    chunks = slots // KC
    cuts = (0, 3, 7, 10, chunks - 1, chunks)
    for low, high in zip(cuts, cuts[1:] + (None,)):
        span = chunks if high is None else min(chunks, high + NEWQ // KC)
        here = tiles > 0
        if low > 0:
            here = here & (edge >= low * KC)
        if high is not None:
            here = here & (edge < high * KC)

        @pl.when(here)
        def _(span=span, clear=low):
            @pl.loop(0, tiles + 1)
            def _(i):
                step(i, span, clear)

    return block


def own_kernel(meta, q_ref, k_ref, vt_ref, o_ref, s, mx, order):
    @pl.loop(0, q_ref.shape[0])
    def _(r):
        sweep(r, r, 0, meta, q_ref, k_ref, vt_ref, o_ref, s, mx, order)


def rest_kernel(req, meta, done_ref, *refs):
    *q_refs, k_ref, vt_ref, o_ref, s, mx, order, q_all = refs
    rows = 2 * TB
    for n, pair in enumerate(q_refs):
        q_all[0, n * rows:(n + 1) * rows, :] = pair[...]
    block = sweep(req, 0, 1, meta, q_all, k_ref, vt_ref, o_ref, s, mx, order)
    for m in range(2):
        at = pl.ds(pl.multiple_of(block(jnp.int32(m - 2)) * TB, TB), TB)
        o_ref[0, at, :] = done_ref[req, m * TB:(m + 1) * TB, :]


def attend(req, meta, qs, keys, turned, done=None):
    width = qs[0].shape[-1]
    slots = keys.shape[1]
    lanes = width // HD * TB
    scratch = [
        pltpu.VMEM((slots, lanes), jnp.float32),
        pltpu.VMEM((8, lanes), jnp.float32),
        pltpu.SMEM((NEWQ // TB,), jnp.int32),
    ]
    if done is None:
        body, shape, extra = own_kernel, qs[0].shape[:2], []
        tiles = shape[0] * 2
    else:
        body, shape, extra = functools.partial(rest_kernel, req), (1, NEWQ), [done]
        tiles = 2 * len(qs)
        scratch.append(pltpu.VMEM((1, tiles * TB, width), jnp.bfloat16))
    return pl.pallas_call(
        body,
        out_shape=jax.ShapeDtypeStruct(shape + (width + HD,), jnp.bfloat16),
        in_specs=[SMEM] + [VMEM] * (len(extra) + len(qs) + 2),
        out_specs=VMEM,
        scratch_shapes=scratch,
        compiler_params=pltpu.CompilerParams(vmem_limit_bytes=40 * 2**20),
        cost_estimate=pl.CostEstimate(
            flops=8 * tiles * lanes * slots * HD, bytes_accessed=4 * 2**20,
            transcendentals=tiles * lanes * slots),
    )(meta, *extra, *qs, keys, turned)


def part_kernel(k_ref, v_ref, keys_ref, turned_ref, flat):
    reqs, n, _ = keys_ref.shape
    flat[0] = k_ref[...].astype(jnp.float32)
    flat[1] = v_ref[...].astype(jnp.float32)
    for r in range(reqs):
        keys_ref[r] = flat[0, pl.ds(r, n, stride=reqs), :].astype(jnp.bfloat16)
        turned_ref[r] = flat[1, pl.ds(r, n, stride=reqs), :].T.astype(jnp.bfloat16)


def part_caches(keys, values):
    slots, reqs, _ = keys.shape
    n = 512
    flat = pl.BlockSpec((n * reqs, HD), lambda i: (i, 0))
    return pl.pallas_call(
        part_kernel,
        grid=(slots // n,),
        out_shape=[
            jax.ShapeDtypeStruct((reqs, slots, HD), jnp.bfloat16),
            jax.ShapeDtypeStruct((reqs, HD, slots), jnp.bfloat16),
        ],
        in_specs=[flat, flat],
        out_specs=[
            pl.BlockSpec((reqs, n, HD), lambda i: (0, i, 0)),
            pl.BlockSpec((reqs, HD, n), lambda i: (0, 0, i)),
        ],
        scratch_shapes=[pltpu.VMEM((2, n * reqs, HD), jnp.float32)],
        compiler_params=pltpu.CompilerParams(vmem_limit_bytes=16 * 2**20),
        cost_estimate=pl.CostEstimate(
            flops=0, bytes_accessed=8 * keys.size, transcendentals=0),
    )(keys.reshape(slots * reqs, HD), values.reshape(slots * reqs, HD))


def merge_kernel(req, meta, part_ref, out_ref, *, cycle, heads):
    srcs, rows = part_ref.shape[0], part_ref.shape[1]
    tps = srcs // cycle
    width = heads * HD
    keep = lax.broadcasted_iota(jnp.int32, (rows, HD), 0) + meta[meta.shape[0] - 1] < meta[(meta.shape[0] - 4) // 2 + req]
    for t in range(tps):
        logs = []
        for c in range(cycle):
            packed = part_ref[c * tps + t, :, width:].astype(jnp.float32)
            logs.append(packed[:, :heads] + packed[:, heads:2 * heads] + packed[:, 2 * heads:3 * heads])
        top = logs[0]
        for ls in logs[1:]:
            top = jnp.maximum(top, ls)
        share = [jnp.exp2(ls - top) for ls in logs]
        total = share[0]
        for s in share[1:]:
            total = total + s
        share = [s / total for s in share]
        for h in range(heads):
            at = slice(h * HD, (h + 1) * HD)
            acc = jnp.zeros((rows, HD), jnp.float32)
            for c in range(cycle):
                acc = acc + share[c][:, h:h + 1] * part_ref[c * tps + t, :, at].astype(jnp.float32)
            out_ref[:, pl.ds(t * width + h * HD, HD)] = jnp.where(keep, acc, 0.0)


def merge(req, meta, parts, cycle, heads):
    srcs, rows, _ = parts.shape
    tps = srcs // cycle
    return pl.pallas_call(
        functools.partial(merge_kernel, req, cycle=cycle, heads=heads),
        out_shape=jax.ShapeDtypeStruct((rows, tps * heads * HD), jnp.float32),
        in_specs=[pl.BlockSpec(memory_space=pltpu.SMEM), pl.BlockSpec(memory_space=pltpu.VMEM)],
        out_specs=pl.BlockSpec(memory_space=pltpu.VMEM),
        compiler_params=pltpu.CompilerParams(vmem_limit_bytes=40 * 2**20),
        cost_estimate=pl.CostEstimate(
            flops=2 * parts.size, bytes_accessed=2 * parts.size, transcendentals=0),
    )(meta, parts)


def shifted(block, across, along):
    size = lax.axis_size("ctx")
    ring = size // 2
    route = [
        (i, (i // ring + across) % 2 * ring + (i % ring + along) % ring) for i in range(size)
    ]
    return lax.ppermute(block, "ctx", route)


def shards(queries, key_cache, value_cache, ctx_len, new_count):
    cycle = lax.axis_size("ctx")
    tps = lax.axis_size("tp")
    here = lax.axis_index("ctx")
    rows, reqs, width = queries.shape
    heads = width // HD
    slots = key_cache.shape[0]
    owners = cycle * tps
    tok_rows = NEWQ // owners
    first_row = (here * tps + lax.axis_index("tp")) * tok_rows
    ring = cycle // 2
    places = jnp.stack([here * slots, here // ring, here % ring, first_row])
    meta = jnp.concatenate([ctx_len, new_count, places])
    split = queries.transpose(1, 0, 2)
    caches = part_caches(key_cache, value_cache)
    other, meta, (keys, turned) = lax.optimization_barrier((shifted(split, 1, 0), meta, caches))
    pairs = jnp.concatenate([split, other], axis=1)
    outs = []
    done = attend(None, meta, [pairs], keys, turned)
    for r in range(reqs):
        qs = [shifted(pairs[r], 0, n) for n in range(1, ring)]
        part = attend(r, meta, qs, keys, turned, done)
        part = part.reshape(owners, tok_rows, width + HD)
        part = lax.all_to_all(part, ("ctx", "tp"), split_axis=0, concat_axis=0)
        outs.append(merge(r, meta, part, cycle, heads))
    return jnp.stack(outs, axis=1).astype(jnp.bfloat16)


def solution(mesh):
    in_specs = (
        P("ctx", "req", "tp"),
        P("ctx", "req", "tp"),
        P("ctx", "req", "tp"),
        P("req"),
        P("req"),
    )
    out_specs = P(("ctx", "tp"), "req", None)
    return jax.shard_map(shards, mesh=mesh, in_specs=in_specs, out_specs=out_specs, check_vma=False)
```

```python
import functools
import math

import jax
import jax.numpy as jnp
from jax import lax
from jax.experimental import pallas as pl
from jax.experimental.pallas import tpu as pltpu
from jax.sharding import PartitionSpec as P

HD = 128
NEWQ = 256
TB = 32
KC = 256
HIDDEN = -1e30
RATE = math.log2(math.e) * HD ** (-0.5)
VMEM = pl.BlockSpec(memory_space=pltpu.VMEM)
SMEM = pl.BlockSpec(memory_space=pltpu.SMEM)


def pack_logs(ls, heads):
    lanes = lax.broadcasted_iota(jnp.int32, ls.shape, 1)
    high = ls.astype(jnp.bfloat16).astype(jnp.float32)
    rest = ls - high
    mid = rest.astype(jnp.bfloat16).astype(jnp.float32)
    packed = jnp.where(lanes < heads, high, jnp.where(lanes < 2 * heads, mid, rest - mid))
    return packed.astype(jnp.bfloat16)


def sweep(req, place, lead, meta, q_ref, k_ref, vt_ref, o_ref, s, mx, order):
    slots = k_ref.shape[1]
    width = q_ref.shape[2]
    heads = width // HD
    lanes = heads * TB
    count = q_ref.shape[1] // TB
    reqs = (meta.shape[0] - 4) // 2
    ring = NEWQ // TB // 2
    ctx_len, new_count, base = meta[req], meta[reqs + req], meta[2 * reqs]
    edge = ctx_len - base + 1
    some = edge + NEWQ - 1 > 0
    of_head = lax.broadcasted_iota(jnp.int32, (TB, HD), 1) % heads
    token = lax.broadcasted_iota(jnp.int32, (1, lanes), 1) % TB
    key = lax.broadcasted_iota(jnp.int32, (KC, lanes), 0)

    def block(j):
        across, along = lax.rem(j, 2), lead + j // 2
        return (meta[2 * reqs + 1] + across) % 2 * ring + (meta[2 * reqs + 2] - along + ring) % ring

    def spot(j):
        return pl.ds(pl.multiple_of((block(j) if lead else j) * TB, TB), TB)

    def note(j, tiles):
        take = some & (block(j) * TB < new_count)

        @pl.when(take)
        def _():
            order[tiles] = j

        @pl.when(jnp.logical_not(take))
        def _():
            none = jnp.full((TB, HD), HIDDEN, jnp.float32)
            o_ref[place, spot(j), :width] = jnp.zeros((TB, width), o_ref.dtype)
            o_ref[place, spot(j), width:] = pack_logs(none, heads)

        return tiles + take.astype(jnp.int32)

    tiles = lax.fori_loop(0, count, note, jnp.int32(0))

    def step(i, span, clear):
        tile = order[jnp.minimum(i, tiles - 1)]
        row = pl.multiple_of(tile * TB, TB)
        q = jnp.concatenate(
            [q_ref[place, pl.ds(row, TB), h * HD:(h + 1) * HD] for h in range(heads)], axis=0)
        shown = edge + block(tile) * TB + token
        shift = jnp.max(mx[...], axis=0, keepdims=True) * RATE
        top = acc = total = None
        for c in range(span):
            at = slice(c * KC, (c + 1) * KC)
            e = jnp.exp2(s[at, :] * RATE - shift)
            part = lax.dot_general(k_ref[req, at, :], q, (((1,), (1,)), ((), ())),
                                   preferred_element_type=jnp.float32)
            if c >= clear:
                part = jnp.where(key < shown - c * KC, part, HIDDEN)
            s[at, :] = part
            high = jnp.max(part.reshape(KC // 8, 8, lanes), axis=0)
            top = high if top is None else jnp.maximum(top, high)
            add = jnp.sum(e.reshape(KC // 8, 8, lanes), axis=0)
            total = add if total is None else total + add
            new = jnp.dot(vt_ref[req, :, at], e.astype(jnp.bfloat16), preferred_element_type=jnp.float32)
            acc = new if acc is None else acc + new
        mx[...] = top
        there = spot(order[jnp.maximum(i - 1, 0)])
        total = jnp.sum(total, axis=0, keepdims=True)
        out = (acc / total).T
        ls = jnp.broadcast_to(shift + jnp.log2(total), (HD, lanes)).T
        kept = jnp.zeros((TB, HD), jnp.float32)
        for h in range(heads):
            at = slice(h * TB, (h + 1) * TB)
            o_ref[place, there, h * HD:(h + 1) * HD] = out[at].astype(o_ref.dtype)
            kept = jnp.where(of_head == h, ls[at], kept)
        o_ref[place, there, width:] = pack_logs(kept, heads)

    chunks = slots // KC
    cuts = (0, 3, 7, 10, chunks - 1, chunks)
    for low, high in zip(cuts, cuts[1:] + (None,)):
        span = chunks if high is None else min(chunks, high + NEWQ // KC)
        here = tiles > 0
        if low > 0:
            here = here & (edge >= low * KC)
        if high is not None:
            here = here & (edge < high * KC)

        @pl.when(here)
        def _(span=span, clear=low):
            @pl.loop(0, tiles + 1)
            def _(i):
                step(i, span, clear)

    return block


def own_kernel(meta, q_ref, k_ref, vt_ref, o_ref, s, mx, order):
    @pl.loop(0, q_ref.shape[0])
    def _(r):
        sweep(r, r, 0, meta, q_ref, k_ref, vt_ref, o_ref, s, mx, order)


def rest_kernel(req, meta, done_ref, *refs):
    *q_refs, k_ref, vt_ref, o_ref, s, mx, order, q_all = refs
    rows = 2 * TB
    for n, pair in enumerate(q_refs):
        q_all[0, n * rows:(n + 1) * rows, :] = pair[...]
    block = sweep(req, 0, 1, meta, q_all, k_ref, vt_ref, o_ref, s, mx, order)
    for m in range(2):
        at = pl.ds(pl.multiple_of(block(jnp.int32(m - 2)) * TB, TB), TB)
        o_ref[0, at, :] = done_ref[req, m * TB:(m + 1) * TB, :]


def attend(req, meta, qs, keys, turned, done=None):
    width = qs[0].shape[-1]
    slots = keys.shape[1]
    lanes = width // HD * TB
    scratch = [
        pltpu.VMEM((slots, lanes), jnp.float32),
        pltpu.VMEM((8, lanes), jnp.float32),
        pltpu.SMEM((NEWQ // TB,), jnp.int32),
    ]
    if done is None:
        body, shape, extra = own_kernel, qs[0].shape[:2], []
        tiles = shape[0] * 2
    else:
        body, shape, extra = functools.partial(rest_kernel, req), (1, NEWQ), [done]
        tiles = 2 * len(qs)
        scratch.append(pltpu.VMEM((1, tiles * TB, width), jnp.bfloat16))
    return pl.pallas_call(
        body,
        out_shape=jax.ShapeDtypeStruct(shape + (width + HD,), jnp.bfloat16),
        in_specs=[SMEM] + [VMEM] * (len(extra) + len(qs) + 2),
        out_specs=VMEM,
        scratch_shapes=scratch,
        compiler_params=pltpu.CompilerParams(vmem_limit_bytes=40 * 2**20),
        cost_estimate=pl.CostEstimate(
            flops=8 * tiles * lanes * slots * HD, bytes_accessed=4 * 2**20,
            transcendentals=tiles * lanes * slots),
    )(meta, *extra, *qs, keys, turned)


def part_kernel(k_ref, v_ref, keys_ref, turned_ref, flat):
    reqs, n, _ = keys_ref.shape
    flat[0] = k_ref[...].astype(jnp.float32)
    flat[1] = v_ref[...].astype(jnp.float32)
    for r in range(reqs):
        keys_ref[r] = flat[0, pl.ds(r, n, stride=reqs), :].astype(jnp.bfloat16)
        turned_ref[r] = flat[1, pl.ds(r, n, stride=reqs), :].T.astype(jnp.bfloat16)


def part_caches(keys, values):
    slots, reqs, _ = keys.shape
    n = 512
    flat = pl.BlockSpec((n * reqs, HD), lambda i: (i, 0))
    return pl.pallas_call(
        part_kernel,
        grid=(slots // n,),
        out_shape=[
            jax.ShapeDtypeStruct((reqs, slots, HD), jnp.bfloat16),
            jax.ShapeDtypeStruct((reqs, HD, slots), jnp.bfloat16),
        ],
        in_specs=[flat, flat],
        out_specs=[
            pl.BlockSpec((reqs, n, HD), lambda i: (0, i, 0)),
            pl.BlockSpec((reqs, HD, n), lambda i: (0, 0, i)),
        ],
        scratch_shapes=[pltpu.VMEM((2, n * reqs, HD), jnp.float32)],
        compiler_params=pltpu.CompilerParams(vmem_limit_bytes=16 * 2**20),
        cost_estimate=pl.CostEstimate(
            flops=0, bytes_accessed=8 * keys.size, transcendentals=0),
    )(keys.reshape(slots * reqs, HD), values.reshape(slots * reqs, HD))


def merge_kernel(req, meta, part_ref, out_ref, *, cycle, heads):
    srcs, rows = part_ref.shape[0], part_ref.shape[1]
    tps = srcs // cycle
    width = heads * HD
    keep = lax.broadcasted_iota(jnp.int32, (rows, HD), 0) + meta[meta.shape[0] - 1] < meta[(meta.shape[0] - 4) // 2 + req]
    for t in range(tps):
        logs = []
        for c in range(cycle):
            packed = part_ref[c * tps + t, :, width:].astype(jnp.float32)
            logs.append(packed[:, :heads] + packed[:, heads:2 * heads] + packed[:, 2 * heads:3 * heads])
        top = logs[0]
        for ls in logs[1:]:
            top = jnp.maximum(top, ls)
        share = [jnp.exp2(ls - top) for ls in logs]
        total = share[0]
        for s in share[1:]:
            total = total + s
        share = [s / total for s in share]
        for h in range(heads):
            at = slice(h * HD, (h + 1) * HD)
            acc = jnp.zeros((rows, HD), jnp.float32)
            for c in range(cycle):
                acc = acc + share[c][:, h:h + 1] * part_ref[c * tps + t, :, at].astype(jnp.float32)
            out_ref[:, pl.ds(t * width + h * HD, HD)] = jnp.where(keep, acc, 0.0)


def merge(req, meta, parts, cycle, heads):
    srcs, rows, _ = parts.shape
    tps = srcs // cycle
    return pl.pallas_call(
        functools.partial(merge_kernel, req, cycle=cycle, heads=heads),
        out_shape=jax.ShapeDtypeStruct((rows, tps * heads * HD), jnp.float32),
        in_specs=[pl.BlockSpec(memory_space=pltpu.SMEM), pl.BlockSpec(memory_space=pltpu.VMEM)],
        out_specs=pl.BlockSpec(memory_space=pltpu.VMEM),
        compiler_params=pltpu.CompilerParams(vmem_limit_bytes=40 * 2**20),
        cost_estimate=pl.CostEstimate(
            flops=2 * parts.size, bytes_accessed=2 * parts.size, transcendentals=0),
    )(meta, parts)


def shifted(block, across, along):
    size = lax.axis_size("ctx")
    ring = size // 2
    route = [
        (i, (i // ring + across) % 2 * ring + (i % ring + along) % ring) for i in range(size)
    ]
    return lax.ppermute(block, "ctx", route)


def shards(queries, key_cache, value_cache, ctx_len, new_count):
    cycle = lax.axis_size("ctx")
    tps = lax.axis_size("tp")
    here = lax.axis_index("ctx")
    rows, reqs, width = queries.shape
    heads = width // HD
    slots = key_cache.shape[0]
    owners = cycle * tps
    tok_rows = NEWQ // owners
    first_row = (here * tps + lax.axis_index("tp")) * tok_rows
    ring = cycle // 2
    places = jnp.stack([here * slots, here // ring, here % ring, first_row])
    meta = jnp.concatenate([ctx_len, new_count, places])
    split = queries.transpose(1, 0, 2)
    caches = part_caches(key_cache, value_cache)
    other, meta, (keys, turned) = lax.optimization_barrier((shifted(queries, 1, 0), meta, caches))
    pairs = jnp.concatenate([split, other.transpose(1, 0, 2)], axis=1)
    outs = []
    done = attend(None, meta, [pairs], keys, turned)
    for r in range(reqs):
        qs = [shifted(pairs[r], 0, n) for n in range(1, ring)]
        part = attend(r, meta, qs, keys, turned, done)
        part = part.reshape(owners, tok_rows, width + HD)
        part = lax.all_to_all(part, ("ctx", "tp"), split_axis=0, concat_axis=0)
        outs.append(merge(r, meta, part, cycle, heads))
    return jnp.stack(outs, axis=1).astype(jnp.bfloat16)


def solution(mesh):
    in_specs = (
        P("ctx", "req", "tp"),
        P("ctx", "req", "tp"),
        P("ctx", "req", "tp"),
        P("req"),
        P("req"),
    )
    out_specs = P(("ctx", "tp"), "req", None)
    return jax.shard_map(shards, mesh=mesh, in_specs=in_specs, out_specs=out_specs, check_vma=False)
```
